128 devices in a mesh: section: 4 (over x), blk: 4 (over z_lo, core), uly: 8 (over z_hi, y).
Axes of the slice: x: 4, y: 4, z: 4 (z_hi: 2, z_lo: 2; z = z_hi * 2 + z_lo), core: 2. Of those that a mesh axis runs over, the one named last changes fastest.
Arguments:
- queries: bfloat16 [4, 4096, 5120], P('section', ('blk', 'uly')), may hold values from -4.5 to 4.5
- keys: bfloat16 [4, 4096, 1024], P('section', ('blk', 'uly')), may hold values from -4.5 to 4.5
- values: bfloat16 [4, 4096, 1024], P('section', ('blk', 'uly')), may hold values from -6 to 6
- pre_keys: bfloat16 [4, 256, 1024], P('section', ('blk', 'uly')), may hold values from -6 to 6
- pre_values: bfloat16 [4, 256, 1024], P('section', ('blk', 'uly')), may hold values from -6 to 6
- d_out: bfloat16 [4, 4096, 5120], P('section', ('blk', 'uly')), may hold values from -6 to 6
- prefix_fill: int32 [4], replicated, may hold values from 1 to 64, 192 in all
Outputs:
- next_input: bfloat16 [4, 4096, 5120], P('section', ('blk', 'uly'))
- query_grad: bfloat16 [4, 4096, 5120], P('section', ('blk', 'uly'))
- key_grad: bfloat16 [4, 4096, 1024], P('section', ('blk', 'uly'))
- value_grad: bfloat16 [4, 4096, 1024], P('section', ('blk', 'uly'))
The draws below stay inside these ranges and needn't reach their ends.
Inputs may be any that keep to these rules, and one draw needn't show every extreme that they name: `prefix_fill`: entry b counts the live rows at the start of prefix block b of 64 rows; some block is full.
All inputs are finite; a program needn't handle non-finite values.
Results may differ from the reference program's by a relative error of at most 0.014.
Values may be sent and summed in bfloat16 or wider, within the bound.
No kernel may reach another device: no remote copies, remote signals or barrier semaphores. Data moves between devices by JAX's collectives and lax.ppermute only.
A program may use at most 128 MiB of HBM per device.

```python
import math
import jax
import jax.numpy as jnp
import numpy as np
from jax import lax

QH = 40
KVH = 8
HD = 128
TOK = 128
SECTIONS = 4
NEW = 4096
PREFIX = 256
PBLK = 64
N_BLK = 4
N_ULY = 8


def draw_queries(key, part):
    key = jax.random.fold_in(key, 11)
    shape = (SECTIONS, NEW, QH * HD)
    base = jnp.clip(jax.random.normal(key, shape, jnp.float32), -4.0, 4.0)
    return base.astype(jnp.bfloat16)


def draw_keys(key, part):
    key = jax.random.fold_in(key, 23)
    shape = (SECTIONS, NEW, KVH * HD)
    base = jnp.clip(jax.random.normal(key, shape, jnp.float32), -4.0, 4.0)
    return base.astype(jnp.bfloat16)


def levels(key, shape, cuts, low, high):
    gain = 1.0
    for dim, shards_of in cuts:
        heights = jax.random.uniform(jax.random.fold_in(jax.random.fold_in(key, 6), dim), (shards_of,), jnp.float32, low / len(cuts), high / len(cuts))
        gain = gain * jnp.repeat(jnp.exp(heights), shape[dim] // shards_of).reshape((-1,) + (1,) * (len(shape) - 1 - dim))
    return gain


def split_up(number_of, total, limit, slope):
    weights = [(1 << 20) // math.isqrt(standing ** slope) + 1 for standing in range(2, number_of + 1)]
    rest, holding = total - limit - (number_of - 1), [1] * (number_of - 1)
    while rest > 0:
        movable = [i for i in range(number_of - 1) if holding[i] < limit]
        pool, remaining = sum([weights[i] for i in movable]), rest
        for i in movable:
            extra = min(limit - holding[i], max(1, remaining * weights[i] // pool), rest)
            holding[i] = holding[i] + extra
            rest = rest - extra
    return np.array([limit] + holding)


def uneven(rng, amount, total, limit, lean):
    if amount == 2:
        one = jax.random.randint(rng, (), max(1, total - limit), min(limit, total - 1) + 1)
        return jnp.stack([one, total - one])
    sizes = jnp.asarray(split_up(amount, total, limit, lean), jnp.int32)
    couples = (amount - 1) // 2
    donor, sink = sizes[1:1 + 2 * couples:2], sizes[2:2 + 2 * couples:2]
    margin = jnp.minimum(donor - 1, limit - sink)
    moved = jax.random.randint(jax.random.fold_in(rng, 1), (couples,), 0, 1 << 20) % (margin + 1)
    sizes = sizes.at[1:1 + 2 * couples:2].set(donor - moved).at[2:2 + 2 * couples:2].set(sink + moved)
    return sizes[jax.random.permutation(jax.random.fold_in(rng, 2), amount)]


def gaussian(key, extent, deviation, limit, pieces=(), kind=jnp.bfloat16):
    array = jax.random.normal(key, extent, jnp.float32) * deviation
    if len(pieces) > 0:
        array = levels(key, extent, pieces, -0.22, 0.18) * array
    return jnp.clip(array, min=-limit, max=limit).astype(kind)


def setup_inputs(seed: int = 0) -> dict:
    key_list = jax.random.split(jax.random.key(seed), 8)
    queries = draw_queries(jax.random.fold_in(key_list[7], 71), 0)
    keys = draw_keys(jax.random.fold_in(key_list[7], 71), 0)
    values = gaussian(key_list[2], (SECTIONS, NEW, KVH * HD), 1.0, 6.0, ((0, 4), (1, 32)))
    pre_keys = gaussian(key_list[3], (SECTIONS, PREFIX, KVH * HD), 1.0, 6.0, ((0, 4), (1, 32)))
    pre_values = gaussian(key_list[4], (SECTIONS, PREFIX, KVH * HD), 1.0, 6.0, ((0, 4), (1, 32)))
    d_out = gaussian(key_list[5], (SECTIONS, NEW, QH * HD), 1.0, 6.0, ((0, 4), (1, 32)))
    prefix_fill = uneven(key_list[6], N_BLK, 3 * PBLK, PBLK, 0).astype(jnp.int32)
    return {"queries": queries, "keys": keys, "values": values, "pre_keys": pre_keys, "pre_values": pre_values, "d_out": d_out, "prefix_fill": prefix_fill}


NEG = -1e+30

def section_pass(queries, keys, values, pre_keys, pre_values, d_out, prefix_fill):
    group = QH // KVH
    scale = 1.0 / math.sqrt(HD)
    block_rows = TOK * N_ULY
    pre_rows = jnp.arange(PREFIX, dtype=jnp.int32)
    pre_live = pre_rows % PBLK < prefix_fill[pre_rows // PBLK]

    def per_group(index):
        key_cols = lax.dynamic_slice_in_dim(keys, index * HD, HD, 1)
        val_cols = lax.dynamic_slice_in_dim(values, index * HD, HD, 1)
        pre_kc = lax.dynamic_slice_in_dim(pre_keys, index * HD, HD, 1)
        pre_vc = lax.dynamic_slice_in_dim(pre_values, index * HD, HD, 1)
        key_total = jnp.zeros((NEW, HD), jnp.float32)
        val_total = jnp.zeros((NEW, HD), jnp.float32)
        out_list = []
        dq_list = []
        for member in range(group):
            head = index * group + member
            q_cols = lax.dynamic_slice_in_dim(queries, head * HD, HD, 1)
            d_cols = lax.dynamic_slice_in_dim(d_out, head * HD, HD, 1)
            out_parts = []
            dq_parts = []
            for block in range(N_BLK):
                first = block * block_rows
                last = first + block_rows
                q_block = q_cols[first:last]
                d_block = d_cols[first:last]
                k_block = jnp.concatenate([pre_kc, key_cols[:last]], axis=0)
                v_block = jnp.concatenate([pre_vc, val_cols[:last]], axis=0)
                causal = jnp.arange(last, dtype=jnp.int32)[None, :] <= (first + jnp.arange(block_rows, dtype=jnp.int32))[:, None]
                live = jnp.concatenate([jnp.broadcast_to(pre_live[None, :], (block_rows, PREFIX)), causal], axis=1)
                score = jnp.dot(q_block, k_block.T, preferred_element_type=jnp.float32) * scale
                score = jnp.where(live, score, NEG)
                top = lax.optimization_barrier(jnp.max(score, axis=-1))
                total = lax.optimization_barrier(jnp.sum(jnp.where(live, jnp.exp(score - top[:, None]), 0.0), axis=-1))
                lse = top + jnp.log(total)
                prob = jnp.where(live, jnp.exp(score - lse[:, None]), 0.0)
                weights = prob.astype(jnp.bfloat16)
                out_block = jnp.dot(weights, v_block, preferred_element_type=jnp.float32).astype(jnp.bfloat16)
                delta = lax.optimization_barrier(jnp.sum(d_block.astype(jnp.float32) * out_block.astype(jnp.float32), axis=-1))
                dprob = jnp.dot(d_block, v_block.T, preferred_element_type=jnp.float32)
                dscore = (prob * (dprob - delta[:, None]) * scale).astype(jnp.bfloat16)
                dq_block = jnp.dot(dscore, k_block, preferred_element_type=jnp.float32).astype(jnp.bfloat16)
                key_total = key_total.at[:last].add(jnp.dot(dscore[:, PREFIX:].T, q_block, preferred_element_type=jnp.float32))
                val_total = val_total.at[:last].add(jnp.dot(weights[:, PREFIX:].T, d_block, preferred_element_type=jnp.float32))
                out_parts.append(out_block)
                dq_parts.append(dq_block)
            out_list.append(jnp.concatenate(out_parts, axis=0))
            dq_list.append(jnp.concatenate(dq_parts, axis=0))
        return (jnp.stack(out_list), jnp.stack(dq_list), key_total.astype(jnp.bfloat16), val_total.astype(jnp.bfloat16))
    outs, dqs, kgrads, vgrads = lax.map(per_group, jnp.arange(KVH, dtype=jnp.int32))
    attn = jnp.transpose(outs, (2, 0, 1, 3)).reshape(NEW, QH * HD)
    qgrad = jnp.transpose(dqs, (2, 0, 1, 3)).reshape(NEW, QH * HD)
    kgrad = jnp.transpose(kgrads, (1, 0, 2)).reshape(NEW, KVH * HD)
    vgrad = jnp.transpose(vgrads, (1, 0, 2)).reshape(NEW, KVH * HD)
    return (attn, qgrad, kgrad, vgrad)

def reference(queries, keys, values, pre_keys, pre_values, d_out, prefix_fill):
    attn_list = []
    qg_list = []
    kg_list = []
    vg_list = []
    for section_index in range(SECTIONS):
        attn, qgrad, kgrad, vgrad = section_pass(queries[section_index], keys[section_index], values[section_index], pre_keys[section_index], pre_values[section_index], d_out[section_index], prefix_fill)
        attn_list.append(attn)
        qg_list.append(qgrad)
        kg_list.append(kgrad)
        vg_list.append(vgrad)
    next_input = jnp.roll(jnp.stack(attn_list), 1, axis=0)
    query_grad = jnp.roll(jnp.stack(qg_list), -1, axis=0)
    key_grad = jnp.roll(jnp.stack(kg_list), -1, axis=0)
    value_grad = jnp.roll(jnp.stack(vg_list), -1, axis=0)
    return (next_input, query_grad, key_grad, value_grad)
```

```python
import math

import jax
import jax.numpy as jnp
import numpy as np
from jax import lax
from jax.experimental import pallas as pl
from jax.experimental.pallas import tpu as pltpu
from jax.sharding import PartitionSpec as P

HD = 128
GROUP = 5
CHUNKS = 32
TOK = 128
SPLIT = 4
SUB = TOK // SPLIT
QR = GROUP * SUB
PRE = 8
K0, V0, P0 = QR, QR + TOK, QR + 2 * TOK
PACK = P0 + 2 * PRE
RC = 8
KC = 4
M = RC * QR
N = KC * TOK
N_RB = CHUNKS // RC
PTOT = CHUNKS * PRE
SCALE = 1.0 / math.sqrt(HD)
SAFE = 60.0
NEG = -1e30
F32 = jnp.float32
BF16 = jnp.bfloat16
VMEM = 60 * 2**20

ROW_OF = np.array([r for r in range(N_RB) for _ in range(2 * r + 2)], np.int32)
KEY_OF = np.array([k for r in range(N_RB) for k in range(2 * r + 2)], np.int32)
STEPS = len(ROW_OF)


def dot(a, b, ca, cb):
    return lax.dot_general(a, b, (((ca,), (cb,)), ((), ())), preferred_element_type=F32)


def wide(x, width):
    return jnp.concatenate([x] * (width // x.shape[1]), axis=1)


def row_pos(first_chunk, chunks, width, part):
    shape = (chunks, GROUP, SUB, width)
    pos = lax.broadcasted_iota(jnp.int32, shape, 0) * TOK + lax.broadcasted_iota(jnp.int32, shape, 2)
    return pos.reshape(chunks * QR, width) + (first_chunk * TOK + part * SUB)


def key_pos(rows, width):
    return lax.broadcasted_iota(jnp.int32, (rows, width), 1)


def prefix_live(fill_ref, rows):
    pos = key_pos(rows, PTOT)
    live = pos < 0
    block = PTOT // SPLIT
    for b in range(SPLIT):
        live = live | ((pos >= b * block) & (pos < b * block + fill_ref[b]))
    return live


def prefix_rows(pack_ref, which):
    both = pack_ref[:, P0:PACK, :].astype(F32)
    return both[:, which * PRE : (which + 1) * PRE].reshape(PTOT, HD).astype(BF16)


def sub_tiles(kind, part):
    def tri(chunk, chunks, width, key_first):
        pos = row_pos(chunk, chunks, width, part)
        return key_pos(chunks * QR, width) + key_first <= pos

    if kind == "full":
        return [(0, M, N, lambda: None)]
    if kind == "first":
        return [
            (0, 2 * QR, N // 2, lambda: tri(0, 2, N // 2, 0)),
            (2 * QR, 4 * QR, N, lambda: tri(2, 2, N, 0)),
            (4 * QR, M, N, lambda: None),
        ]
    return [
        (4 * QR, 6 * QR, N // 2, lambda: tri(4, 2, N // 2, N)),
        (6 * QR, M, N, lambda: tri(6, 2, N, N)),
    ]


def forward_kernel(row_of, key_of, meta, pack, e_out, ep_out, o_out, li_out, acc, shift, pk, pv, knorm):
    t = pl.program_id(0)
    rb, kb = row_of[t], key_of[t]
    part = meta[SPLIT]

    @pl.when(t == 0)
    def _():
        pk[...] = prefix_rows(pack, 0)
        pv[...] = prefix_rows(pack, 1)
        top = jnp.max(jnp.sum(jnp.square(pk[...].astype(F32)), axis=1))

        def step(c, best):
            rows = pack[c, K0:V0, :].astype(F32)
            return jnp.maximum(best, jnp.max(jnp.sum(rows * rows, axis=1)))

        knorm[0] = lax.fori_loop(0, CHUNKS, step, top)

    def queries():
        return pack[pl.ds(rb * RC, RC), 0:QR, :].reshape(M, HD)

    @pl.when(kb == 0)
    def _():
        acc[...] = jnp.zeros_like(acc)
        shift[...] = jnp.zeros_like(shift)
        q = queries()
        qf = q.astype(F32)
        qnorm = jnp.max(jnp.sum(qf * qf, axis=1))

        @pl.when(jnp.logical_not(qnorm * knorm[0] * (SCALE * SCALE) <= SAFE * SAFE))
        def _():
            live = prefix_live(meta, M)
            s = jnp.where(live, dot(q, pk[...], 1, 1) * SCALE, NEG)
            shift[...] = jnp.broadcast_to(jnp.max(s, axis=1, keepdims=True), shift.shape)

            def step(k, carry):
                keys = pack[pl.ds(k * KC, KC), K0:V0, :].reshape(N, HD)
                pos = row_pos(0, RC, N, part) + rb * (RC * TOK)
                s = jnp.where(key_pos(M, N) + k * N <= pos, dot(q, keys, 1, 1) * SCALE, NEG)
                top = jnp.broadcast_to(jnp.max(s, axis=1, keepdims=True), shift.shape)
                shift[...] = jnp.maximum(shift[...], top)
                return carry

            lax.fori_loop(0, 2 * rb + 2, step, 0)

    def tile(first, last, keys, values, live, store):
        width = keys.shape[0]
        q = pack[pl.ds(rb * RC + first // QR, (last - first) // QR), 0:QR, :].reshape(last - first, HD)
        s = dot(q, keys, 1, 1) * SCALE - wide(shift[first:last, :], width)
        e = jnp.exp(s)
        if live is not None:
            e = jnp.where(live, e, 0.0)
        e = e.astype(BF16)
        store[0, first:last, 0:width] = e
        both = jnp.concatenate([values, jnp.ones_like(values)], axis=1)
        acc[first:last, :] += dot(e, both, 1, 0)

    keys = lambda n: pack[pl.ds(kb * KC, n // TOK), K0:V0, :].reshape(n, HD)
    values = lambda n: pack[pl.ds(kb * KC, n // TOK), V0:P0, :].reshape(n, HD)

    @pl.when(kb < 2 * rb)
    def _():
        for first, last, n, live in sub_tiles("full", part):
            tile(first, last, keys(n), values(n), live(), e_out)

    @pl.when(kb == 2 * rb)
    def _():
        for first, last, n, live in sub_tiles("first", part):
            tile(first, last, keys(n), values(n), live(), e_out)

    @pl.when(kb == 2 * rb + 1)
    def _():
        for first, last, n, live in sub_tiles("second", part):
            tile(first, last, keys(n), values(n), live(), e_out)
        tile(0, M, pk[...], pv[...], prefix_live(meta, M), ep_out)
        inverse = 1.0 / acc[:, HD:]
        li_out[...] = inverse
        o_out[...] = (acc[:, :HD] * inverse).astype(BF16).reshape(RC, QR, HD)


def forward(meta, pack):
    whole = lambda *shape: pl.BlockSpec(shape, lambda t, r, k, m: (0,) * len(shape))
    return pl.pallas_call(
        forward_kernel,
        grid_spec=pltpu.PrefetchScalarGridSpec(
            num_scalar_prefetch=3,
            grid=(STEPS,),
            in_specs=[whole(CHUNKS, PACK, HD)],
            out_specs=[
                pl.BlockSpec((1, M, N), lambda t, r, k, m: (t, 0, 0)),
                pl.BlockSpec((1, M, PTOT), lambda t, r, k, m: (r[t], 0, 0)),
                pl.BlockSpec((RC, QR, HD), lambda t, r, k, m: (r[t], 0, 0)),
                pl.BlockSpec((M, HD), lambda t, r, k, m: (r[t], 0)),
            ],
            scratch_shapes=[
                pltpu.VMEM((M, 2 * HD), F32),
                pltpu.VMEM((M, HD), F32),
                pltpu.VMEM((PTOT, HD), BF16),
                pltpu.VMEM((PTOT, HD), BF16),
                pltpu.SMEM((1,), F32),
            ],
        ),
        out_shape=[
            jax.ShapeDtypeStruct((STEPS, M, N), BF16),
            jax.ShapeDtypeStruct((N_RB, M, PTOT), BF16),
            jax.ShapeDtypeStruct((CHUNKS, QR, HD), BF16),
            jax.ShapeDtypeStruct((N_RB * M, HD), F32),
        ],
        compiler_params=pltpu.CompilerParams(vmem_limit_bytes=VMEM),
        name="forward",
    )(jnp.asarray(ROW_OF), jnp.asarray(KEY_OF), meta, pack)


def backward_kernel(row_of, key_of, meta, pack, d_in, e_in, ep_in, o_in, li_in, dq_out, dkv_out, dq, dk, dv, dn, delta, pk, pv):
    t = pl.program_id(0)
    rb, kb = row_of[t], key_of[t]
    part = meta[SPLIT]

    @pl.when(t == 0)
    def _():
        pk[...] = prefix_rows(pack, 0)
        pv[...] = prefix_rows(pack, 1)
        dk[...] = jnp.zeros_like(dk)
        dv[...] = jnp.zeros_like(dv)

    @pl.when(kb == 0)
    def _():
        dq[...] = jnp.zeros_like(dq)
        d = d_in[...].reshape(M, HD).astype(F32) * (li_in[...] * SCALE)
        d = d.astype(BF16)
        dn[...] = d
        total = jnp.sum(d.astype(F32) * o_in[...].reshape(M, HD).astype(F32), axis=1, keepdims=True)
        delta[...] = jnp.broadcast_to(total, delta.shape)

    def tile(first, last, keys, values, e_ref, grads):
        width = keys.shape[0]
        q = pack[pl.ds(rb * RC + first // QR, (last - first) // QR), 0:QR, :].reshape(last - first, HD)
        d = dn[first:last, :]
        e = e_ref[0, first:last, 0:width]
        dp = dot(d, values, 1, 1) - wide(delta[first:last, :], width)
        ds = (e.astype(F32) * dp).astype(BF16)
        dq[first:last, :] += dot(ds, keys, 1, 0)
        if grads:
            at = pl.ds(kb * N, width)
            dv[at, :] += dot(e, d, 0, 0)
            dk[at, :] += dot(ds, q, 0, 0)

    keys = lambda n: pack[pl.ds(kb * KC, n // TOK), K0:V0, :].reshape(n, HD)
    values = lambda n: pack[pl.ds(kb * KC, n // TOK), V0:P0, :].reshape(n, HD)

    @pl.when(kb < 2 * rb)
    def _():
        for first, last, n, live in sub_tiles("full", part):
            tile(first, last, keys(n), values(n), e_in, True)

    @pl.when(kb == 2 * rb)
    def _():
        for first, last, n, live in sub_tiles("first", part):
            tile(first, last, keys(n), values(n), e_in, True)

    @pl.when(kb == 2 * rb + 1)
    def _():
        for first, last, n, live in sub_tiles("second", part):
            tile(first, last, keys(n), values(n), e_in, True)
        tile(0, M, pk[...], pv[...], ep_in, False)
        dq_out[...] = dq[...].astype(BF16).reshape(RC, QR, HD)

    @pl.when(t == STEPS - 1)
    def _():
        dkv_out[:, 0:TOK, :] = dk[...].astype(BF16).reshape(CHUNKS, TOK, HD)
        dkv_out[:, TOK:, :] = (dv[...] * (1.0 / SCALE)).astype(BF16).reshape(CHUNKS, TOK, HD)


def backward(meta, pack, d, e, ep, o, li):
    whole = lambda *shape: pl.BlockSpec(shape, lambda t, r, k, m: (0,) * len(shape))
    by_rows = lambda *shape: pl.BlockSpec(shape, lambda t, r, k, m: (r[t],) + (0,) * (len(shape) - 1))
    return pl.pallas_call(
        backward_kernel,
        grid_spec=pltpu.PrefetchScalarGridSpec(
            num_scalar_prefetch=3,
            grid=(STEPS,),
            in_specs=[
                whole(CHUNKS, PACK, HD),
                by_rows(RC, QR, HD),
                pl.BlockSpec((1, M, N), lambda t, r, k, m: (t, 0, 0)),
                by_rows(1, M, PTOT),
                by_rows(RC, QR, HD),
                by_rows(M, HD),
            ],
            out_specs=[by_rows(RC, QR, HD), whole(CHUNKS, 2 * TOK, HD)],
            scratch_shapes=[
                pltpu.VMEM((M, HD), F32),
                pltpu.VMEM((CHUNKS * TOK, HD), F32),
                pltpu.VMEM((CHUNKS * TOK, HD), F32),
                pltpu.VMEM((M, HD), BF16),
                pltpu.VMEM((M, HD), F32),
                pltpu.VMEM((PTOT, HD), BF16),
                pltpu.VMEM((PTOT, HD), BF16),
            ],
        ),
        out_shape=[
            jax.ShapeDtypeStruct((CHUNKS, QR, HD), BF16),
            jax.ShapeDtypeStruct((CHUNKS, 2 * TOK, HD), BF16),
        ],
        compiler_params=pltpu.CompilerParams(vmem_limit_bytes=VMEM),
        name="backward",
    )(jnp.asarray(ROW_OF), jnp.asarray(KEY_OF), meta, pack, d, e, ep, o, li)


def to_groups(x):
    x = x.reshape(SPLIT, SUB, -1, GROUP, HD)
    return jnp.transpose(x, (0, 2, 3, 1, 4)).reshape(CHUNKS, QR, HD)


def to_tokens(x):
    x = x.reshape(SPLIT, -1, GROUP, SUB, HD)
    return jnp.transpose(x, (0, 3, 1, 2, 4)).reshape(TOK, -1)


def key_groups(x):
    rows = x.shape[0]
    x = jnp.transpose(x.reshape(rows, -1, HD), (1, 0, 2))
    return jnp.broadcast_to(x[None], (SPLIT,) + x.shape).reshape(CHUNKS, rows, HD)


def exchange(x):
    return lax.all_to_all(x, ("blk", "uly"), split_axis=0, concat_axis=0, tiled=True)


def shifted(block, distance):
    count = lax.axis_size("section")
    return lax.ppermute(block, "section", [((i - distance) % count, i) for i in range(count)])


def shards(queries, keys, values, pre_keys, pre_values, d_out, prefix_fill):
    part = lax.axis_index("blk").astype(jnp.int32)
    meta = jnp.concatenate([prefix_fill, part[None]])
    sent = jnp.concatenate(
        [to_groups(queries[0])] + [key_groups(x[0]) for x in (keys, values, pre_keys, pre_values)], axis=1
    )
    pack = exchange(sent)
    d = exchange(to_groups(d_out[0]))
    e, ep, o, li = forward(meta, pack)
    moved_out = shifted(to_tokens(exchange(o)), 1)
    dq, dkv = backward(meta, pack, d, e, ep, o, li)
    moved_q = shifted(to_tokens(exchange(dq)), -1)
    parts = exchange(dkv).reshape(SPLIT, -1, 2, TOK, HD).astype(F32).sum(axis=0).astype(BF16)
    sums = jnp.transpose(parts, (1, 2, 0, 3)).reshape(2, TOK, -1)
    moved_kv = shifted(sums, -1)
    return (moved_out[None], moved_q[None], moved_kv[0][None], moved_kv[1][None])


def solution(mesh):
    spec = P("section", ("blk", "uly"), None)
    return jax.shard_map(
        shards,
        mesh=mesh,
        in_specs=(spec,) * 6 + (P(),),
        out_specs=(spec,) * 4,
        check_vma=False,
    )
```

```python
import math

import jax
import jax.numpy as jnp
import numpy as np
from jax import lax
from jax.experimental import pallas as pl
from jax.experimental.pallas import tpu as pltpu
from jax.sharding import PartitionSpec as P

HD = 128
GROUP = 5
CHUNKS = 32
TOK = 128
SPLIT = 4
SUB = TOK // SPLIT
QR = GROUP * SUB
PRE = 8
K0, V0, P0 = QR, QR + TOK, QR + 2 * TOK
PACK = P0 + 2 * PRE
RC = 8
KC = 4
M = RC * QR
N = KC * TOK
HALF = M // 2
N_RB = CHUNKS // RC
PTOT = CHUNKS * PRE
SCALE = 1.0 / math.sqrt(HD)
SAFE = 60.0
NEG = -1e30
F32 = jnp.float32
BF16 = jnp.bfloat16
VMEM = 40 * 2**20

ROW_OF = np.array([r for r in reversed(range(N_RB)) for _ in range(2 * r + 2)], np.int32)
KEY_OF = np.array([k for r in reversed(range(N_RB)) for k in range(2 * r + 2)], np.int32)
STEPS = len(ROW_OF)


def COST(products):
    entries = (STEPS + N_RB) * M * N
    return pl.CostEstimate(
        flops=products * 2 * entries * HD, transcendentals=entries, bytes_accessed=products * entries
    )


def dot(a, b, ca, cb):
    return lax.dot_general(a, b, (((ca,), (cb,)), ((), ())), preferred_element_type=F32)


def wide(x, width):
    return jnp.concatenate([x] * (width // x.shape[1]), axis=1)


def row_norm(x):
    return jnp.max(dot(x * x, jnp.ones((HD, HD), BF16), 1, 0))


def row_pos(chunks, width, part):
    shape = (chunks, GROUP, SUB, width)
    pos = lax.broadcasted_iota(jnp.int32, shape, 0) * TOK + lax.broadcasted_iota(jnp.int32, shape, 2)
    return pos.reshape(chunks * QR, width) + part * SUB


def key_pos(rows, width):
    return lax.broadcasted_iota(jnp.int32, (rows, width), 1)


def prefix_live(fill_ref, rows):
    pos = key_pos(rows, PTOT)
    live = pos < 0
    block = PTOT // SPLIT
    for b in range(SPLIT):
        live = live | ((pos >= b * block) & (pos < b * block + fill_ref[b]))
    return live


def prefix_rows(pack_ref, which):
    both = pack_ref[:, P0:PACK, :].astype(F32)
    return both[:, which * PRE : (which + 1) * PRE].reshape(PTOT, HD).astype(BF16)


def forward_kernel(row_of, key_of, meta, pack, e_out, o_out, li_out, acc, shift, pk, pv, knorm):
    t = pl.program_id(0)
    rb, kb = row_of[t], key_of[t]
    part = meta[SPLIT]

    @pl.when(t == 0)
    def _():
        pk[...] = prefix_rows(pack, 0)
        pv[...] = prefix_rows(pack, 1)
        knorm[0] = jnp.maximum(row_norm(pk[...]), row_norm(pack[:, K0:V0, :].reshape(CHUNKS * TOK, HD)))

    def queries():
        return pack[pl.ds(rb * RC, RC), 0:QR, :].reshape(M, HD)

    @pl.when(kb == 0)
    def _():
        acc[...] = jnp.zeros_like(acc)
        shift[...] = jnp.zeros_like(shift)
        q = queries()
        qnorm = row_norm(q)

        @pl.when(jnp.logical_not(qnorm * knorm[0] * (SCALE * SCALE) <= SAFE * SAFE))
        def _():
            live = prefix_live(meta, M)
            s = jnp.where(live, dot(q, pk[...], 1, 1) * SCALE, NEG)
            shift[...] = jnp.broadcast_to(jnp.max(s, axis=1, keepdims=True), shift.shape)

            def step(k, carry):
                keys = pack[pl.ds(k * KC, KC), K0:V0, :].reshape(N, HD)
                pos = row_pos(RC, N, part) + rb * (RC * TOK)
                s = jnp.where(key_pos(M, N) + k * N <= pos, dot(q, keys, 1, 1) * SCALE, NEG)
                top = jnp.broadcast_to(jnp.max(s, axis=1, keepdims=True), shift.shape)
                shift[...] = jnp.maximum(shift[...], top)
                return carry

            lax.fori_loop(0, 2 * rb + 2, step, 0)

    def tile(first, keys, values, live=None, at=None):
        width = keys.shape[0]
        row, col = at or (first, 0)
        q = pack[pl.ds(rb * RC + first // QR, RC // 2), 0:QR, :].reshape(HALF, HD)
        e = jnp.exp(dot(q, keys, 1, 1) * SCALE - wide(shift[first : first + HALF, :], width))
        if live is not None:
            e = jnp.where(live, e, 0.0)
        e = e.astype(BF16)
        e_out[0, row : row + HALF, col : col + width] = e
        both = jnp.concatenate([values, jnp.ones_like(values)], axis=1)
        acc[first : first + HALF, :] += dot(e, both, 1, 0)

    keys = pack[pl.ds(kb * KC, KC), K0:V0, :].reshape(N, HD)
    values = pack[pl.ds(kb * KC, KC), V0:P0, :].reshape(N, HD)
    causal = lambda: key_pos(HALF, N) <= row_pos(RC // 2, N, part)

    @pl.when(kb < 2 * rb)
    def _():
        tile(0, keys, values)

    @pl.when(kb <= 2 * rb)
    def _():
        tile(HALF, keys, values)

    @pl.when(kb == 2 * rb)
    def _():
        tile(0, keys, values, causal())

    @pl.when(kb == 2 * rb + 1)
    def _():
        tile(HALF, keys, values, causal())
        live = prefix_live(meta, HALF)
        for half in range(2):
            tile(half * HALF, pk[...], pv[...], live, (0, half * PTOT))
        inverse = 1.0 / acc[:, HD:]
        li_out[...] = inverse
        o_out[...] = (acc[:, :HD] * inverse).astype(BF16).reshape(RC, QR, HD)


def forward(meta, pack):
    return pl.pallas_call(
        forward_kernel,
        grid_spec=pltpu.PrefetchScalarGridSpec(
            num_scalar_prefetch=3,
            grid=(STEPS,),
            in_specs=[pl.BlockSpec(memory_space=pltpu.VMEM)],
            out_specs=[
                pl.BlockSpec((1, M, N), lambda t, r, k, m: (t, 0, 0)),
                pl.BlockSpec((RC, QR, HD), lambda t, r, k, m: (r[t], 0, 0)),
                pl.BlockSpec((M, HD), lambda t, r, k, m: (r[t], 0)),
            ],
            scratch_shapes=[
                pltpu.VMEM((M, 2 * HD), F32),
                pltpu.VMEM((M, HD), F32),
                pltpu.VMEM((PTOT, HD), BF16),
                pltpu.VMEM((PTOT, HD), BF16),
                pltpu.SMEM((1,), F32),
            ],
        ),
        out_shape=[
            jax.ShapeDtypeStruct((STEPS, M, N), BF16),
            jax.ShapeDtypeStruct((CHUNKS, QR, HD), BF16),
            jax.ShapeDtypeStruct((N_RB * M, HD), F32),
        ],
        compiler_params=pltpu.CompilerParams(vmem_limit_bytes=VMEM),
        cost_estimate=COST(2),
        name="forward",
    )(jnp.asarray(ROW_OF), jnp.asarray(KEY_OF), meta, pack)


def backward_kernel(row_of, key_of, meta, pack, d_in, e_in, o_in, li_in, dq_out, dkv_out, dq, dk, dv, dn, delta, pk, pv):
    t = pl.program_id(0)
    rb, kb = row_of[t], key_of[t]
    part = meta[SPLIT]

    @pl.when(t == 0)
    def _():
        pk[...] = prefix_rows(pack, 0)
        pv[...] = prefix_rows(pack, 1)

    @pl.when(kb == 0)
    def _():
        dq[...] = jnp.zeros_like(dq)
        d = (d_in[...].reshape(M, HD).astype(F32) * (li_in[...] * SCALE)).astype(BF16)
        dn[...] = d
        total = jnp.sum(d.astype(F32) * o_in[...].reshape(M, HD).astype(F32), axis=1, keepdims=True)
        delta[...] = jnp.broadcast_to(total, delta.shape)

    here = pl.ds(kb * N, N)

    @pl.when(rb == N_RB - 1)
    def _():
        dk[here, :] = jnp.zeros((N, HD), F32)
        dv[here, :] = jnp.zeros((N, HD), F32)

    def tile(first, keys, values, at=None):
        width = keys.shape[0]
        row, col = at or (first, 0)
        d = dn[first : first + HALF, :]
        e = e_in[0, row : row + HALF, col : col + width]
        dp = dot(d, values, 1, 1) - wide(delta[first : first + HALF, :], width)
        ds = (e.astype(F32) * dp).astype(BF16)
        dq[first : first + HALF, :] += dot(ds, keys, 1, 0)
        if at is None:
            q = pack[pl.ds(rb * RC + first // QR, RC // 2), 0:QR, :].reshape(HALF, HD)
            dv[here, :] += dot(e, d, 0, 0)
            dk[here, :] += dot(ds, q, 0, 0)

    keys = pack[pl.ds(kb * KC, KC), K0:V0, :].reshape(N, HD)
    values = pack[pl.ds(kb * KC, KC), V0:P0, :].reshape(N, HD)

    @pl.when(kb <= 2 * rb)
    def _():
        tile(0, keys, values)

    tile(HALF, keys, values)

    @pl.when(kb == 2 * rb + 1)
    def _():
        for half in range(2):
            tile(half * HALF, pk[...], pv[...], (0, half * PTOT))
        dq_out[...] = dq[...].astype(BF16).reshape(RC, QR, HD)

    @pl.when(kb >= 2 * rb)
    def _():
        dkv_out[:, 0:TOK, :] = dk[here, :].astype(BF16).reshape(KC, TOK, HD)
        dkv_out[:, TOK:, :] = (dv[here, :] * (1.0 / SCALE)).astype(BF16).reshape(KC, TOK, HD)


def backward(meta, pack, d, e, o, li):
    by_rows = lambda *shape: pl.BlockSpec(shape, lambda t, r, k, m: (r[t],) + (0,) * (len(shape) - 1))
    return pl.pallas_call(
        backward_kernel,
        grid_spec=pltpu.PrefetchScalarGridSpec(
            num_scalar_prefetch=3,
            grid=(STEPS,),
            in_specs=[
                pl.BlockSpec(memory_space=pltpu.VMEM),
                by_rows(RC, QR, HD),
                pl.BlockSpec((1, M, N), lambda t, r, k, m: (t, 0, 0)),
                by_rows(RC, QR, HD),
                by_rows(M, HD),
            ],
            out_specs=[
                by_rows(RC, QR, HD),
                pl.BlockSpec((KC, 2 * TOK, HD), lambda t, r, k, m: (jnp.maximum(k[t], 2 * r[t]), 0, 0)),
            ],
            scratch_shapes=[
                pltpu.VMEM((M, HD), F32),
                pltpu.VMEM((CHUNKS * TOK, HD), F32),
                pltpu.VMEM((CHUNKS * TOK, HD), F32),
                pltpu.VMEM((M, HD), BF16),
                pltpu.VMEM((M, HD), F32),
                pltpu.VMEM((PTOT, HD), BF16),
                pltpu.VMEM((PTOT, HD), BF16),
            ],
        ),
        out_shape=[
            jax.ShapeDtypeStruct((CHUNKS, QR, HD), BF16),
            jax.ShapeDtypeStruct((CHUNKS, 2 * TOK, HD), BF16),
        ],
        compiler_params=pltpu.CompilerParams(vmem_limit_bytes=VMEM),
        cost_estimate=COST(4),
        name="backward",
    )(jnp.asarray(ROW_OF), jnp.asarray(KEY_OF), meta, pack, d, e, o, li)


GROUPS = CHUNKS // SPLIT
AT_ONCE = 4


def cols(rows, width):
    return pl.BlockSpec((1, rows, AT_ONCE * width), lambda g: (0, 0, g))


def parts_of(rows):
    return pl.BlockSpec((SPLIT, AT_ONCE, rows, HD), lambda g: (0, g, 0, 0))


def each_head():
    for g in range(AT_ONCE):
        for h in range(GROUP):
            at = (g * GROUP + h) * HD
            yield g, slice(h * SUB, (h + 1) * SUB), slice(at, at + HD)


def gather_kernel(*refs):
    queries, rest, out = refs[0], refs[1:-1], refs[-1]
    for j in range(SPLIT):
        for g, rows, at in each_head():
            out[j, g, rows, :] = queries[0, j * SUB : (j + 1) * SUB, at]
    if rest:
        keys, values, pre_keys, pre_values = rest
        for g in range(AT_ONCE):
            at = slice(g * HD, (g + 1) * HD)
            prefix = jnp.concatenate([pre_keys[0, :, at].astype(F32), pre_values[0, :, at].astype(F32)], axis=0)
            prefix = prefix.astype(BF16)
            for j in range(SPLIT):
                out[j, g, K0:V0, :] = keys[0, :, at]
                out[j, g, V0:P0, :] = values[0, :, at]
                out[j, g, P0:PACK, :] = prefix


def gather(queries, *rest):
    rows = PACK if rest else QR
    packed = pl.pallas_call(
        gather_kernel,
        grid=(GROUPS // AT_ONCE,),
        in_specs=[cols(x.shape[1], x.shape[2] // GROUPS) for x in (queries,) + rest],
        out_specs=parts_of(rows),
        out_shape=jax.ShapeDtypeStruct((SPLIT, GROUPS, rows, HD), BF16),
        compiler_params=pltpu.CompilerParams(vmem_limit_bytes=VMEM),
        name="gather",
    )(queries, *rest)
    return packed.reshape(CHUNKS, rows, HD)


def spread_kernel(packed, out):
    for j in range(SPLIT):
        for g, rows, at in each_head():
            out[0, j * SUB : (j + 1) * SUB, at] = packed[j, g, rows, :]


def spread(packed):
    return pl.pallas_call(
        spread_kernel,
        grid=(GROUPS // AT_ONCE,),
        in_specs=[parts_of(QR)],
        out_specs=cols(TOK, GROUP * HD),
        out_shape=jax.ShapeDtypeStruct((1, TOK, GROUPS * GROUP * HD), BF16),
        compiler_params=pltpu.CompilerParams(vmem_limit_bytes=VMEM),
        name="spread",
    )(packed.reshape(SPLIT, GROUPS, QR, HD))


def sum_kernel(parts, keys, values):
    for g in range(AT_ONCE):
        total = parts[0, g].astype(F32)
        for j in range(1, SPLIT):
            total += parts[j, g].astype(F32)
        keys[0, :, g * HD : (g + 1) * HD] = total[:TOK].astype(BF16)
        values[0, :, g * HD : (g + 1) * HD] = total[TOK:].astype(BF16)


def sum_parts(parts):
    shape = jax.ShapeDtypeStruct((1, TOK, GROUPS * HD), BF16)
    return pl.pallas_call(
        sum_kernel,
        grid=(GROUPS // AT_ONCE,),
        in_specs=[parts_of(2 * TOK)],
        out_specs=[cols(TOK, HD), cols(TOK, HD)],
        out_shape=[shape, shape],
        compiler_params=pltpu.CompilerParams(vmem_limit_bytes=VMEM),
        name="sum_parts",
    )(parts.reshape(SPLIT, GROUPS, 2 * TOK, HD))


def exchange(x):
    return lax.all_to_all(x, ("blk", "uly"), split_axis=0, concat_axis=0, tiled=True)


def shifted(block, distance):
    count = lax.axis_size("section")
    return lax.ppermute(block, "section", [((i - distance) % count, i) for i in range(count)])


def shards(queries, keys, values, pre_keys, pre_values, d_out, prefix_fill):
    part = lax.axis_index("blk").astype(jnp.int32)
    meta = jnp.concatenate([prefix_fill, part[None]])
    pack = exchange(gather(queries, keys, values, pre_keys, pre_values))
    d = exchange(gather(d_out))
    pack = pltpu.with_memory_space_constraint(pack, pltpu.VMEM)
    e, o, li = forward(meta, pack)
    next_input = shifted(spread(exchange(o)), 1)
    dq, dkv = backward(meta, pack, d, e, o, li)
    query_grad = spread(exchange(shifted(dq, -1)))
    key_grad, value_grad = (shifted(x, -1) for x in sum_parts(exchange(dkv)))
    return (next_input, query_grad, key_grad, value_grad)


def solution(mesh):
    spec = P("section", ("blk", "uly"), None)
    return jax.shard_map(
        shards,
        mesh=mesh,
        in_specs=(spec,) * 6 + (P(),),
        out_specs=(spec,) * 4,
        check_vma=False,
    )
```

```python
import math

import jax
import jax.numpy as jnp
import numpy as np
from jax import lax
from jax.experimental import pallas as pl
from jax.experimental.pallas import tpu as pltpu
from jax.sharding import PartitionSpec as P

HD = 128
GROUP = 5
CHUNKS = 32
TOK = 128
SPLIT = 4
SUB = TOK // SPLIT
QR = GROUP * SUB
PRE = 8
K0, V0, P0 = QR, QR + TOK, QR + 2 * TOK
PACK = P0 + 2 * PRE
RC = 8
KC = 8
M = RC * QR
N = KC * TOK
HALF = M // 2
FULL = HALF
N_RB = CHUNKS // RC
PTOT = CHUNKS * PRE
SCALE = 1.0 / math.sqrt(HD)
SAFE = 60.0
NEG = -1e30
F32 = jnp.float32
BF16 = jnp.bfloat16
VMEM = 56 * 2**20

ROW_OF = np.array([r for r in reversed(range(N_RB)) for _ in range(r + 1)], np.int32)
KEY_OF = np.array([k for r in reversed(range(N_RB)) for k in range(r + 1)], np.int32)
STEPS = len(ROW_OF)


def COST(products):
    entries = STEPS * M * N
    return pl.CostEstimate(
        flops=products * 2 * entries * HD, transcendentals=entries, bytes_accessed=products * entries
    )


def in_hbm(*arrays):
    return tuple(pltpu.with_memory_space_constraint(x, pltpu.HBM) for x in arrays)


def dot(a, b, ca, cb):
    return lax.dot_general(a, b, (((ca,), (cb,)), ((), ())), preferred_element_type=F32)


def wide(x, width):
    return jnp.concatenate([x] * (width // x.shape[1]), axis=1)


def row_norm(x):
    return jnp.max(dot(x * x, jnp.ones((HD, HD), BF16), 1, 0))


def row_pos(chunks, width, part):
    shape = (chunks, GROUP, SUB, width)
    pos = lax.broadcasted_iota(jnp.int32, shape, 0) * TOK + lax.broadcasted_iota(jnp.int32, shape, 2)
    return pos.reshape(chunks * QR, width) + part * SUB


def key_pos(rows, width):
    return lax.broadcasted_iota(jnp.int32, (rows, width), 1)


def prefix_live(fill_ref, rows):
    pos = key_pos(rows, PTOT)
    live = pos < 0
    block = PTOT // SPLIT
    for b in range(SPLIT):
        live = live | ((pos >= b * block) & (pos < b * block + fill_ref[b]))
    return live


def prefix_rows(pack_ref, which):
    both = pack_ref[:, P0:PACK, :].astype(F32)
    return both[:, which * PRE : (which + 1) * PRE].reshape(PTOT, HD).astype(BF16)


def forward_kernel(row_of, key_of, meta, pack, e_out, o_out, li_out, acc, shift, pk, pv, knorm):
    t = pl.program_id(0)
    rb, kb = row_of[t], key_of[t]
    part = meta[SPLIT]

    @pl.when(t == 0)
    def _():
        pk[...] = prefix_rows(pack, 0)
        pv[...] = prefix_rows(pack, 1)
        knorm[0] = jnp.maximum(row_norm(pk[...]), row_norm(pack[:, K0:V0, :].reshape(CHUNKS * TOK, HD)))

    def queries():
        return pack[pl.ds(rb * RC, RC), 0:QR, :].reshape(M, HD)

    @pl.when(kb == 0)
    def _():
        acc[...] = jnp.zeros_like(acc)
        shift[...] = jnp.zeros_like(shift)
        q = queries()
        qnorm = row_norm(q)

        @pl.when(jnp.logical_not(qnorm * knorm[0] * (SCALE * SCALE) <= SAFE * SAFE))
        def _():
            live = prefix_live(meta, M)
            s = jnp.where(live, dot(q, pk[...], 1, 1) * SCALE, NEG)
            shift[...] = jnp.broadcast_to(jnp.max(s, axis=1, keepdims=True), shift.shape)

            def step(k, carry):
                keys = pack[pl.ds(k * KC, KC), K0:V0, :].reshape(N, HD)
                pos = row_pos(RC, N, part) + rb * (RC * TOK)
                s = jnp.where(key_pos(M, N) + k * N <= pos, dot(q, keys, 1, 1) * SCALE, NEG)
                top = jnp.broadcast_to(jnp.max(s, axis=1, keepdims=True), shift.shape)
                shift[...] = jnp.maximum(shift[...], top)
                return carry

            lax.fori_loop(0, rb + 1, step, 0)

    def tile(first, rows, keys, values, live=None, at=None):
        width = keys.shape[0]
        row, col = at or (first, 0)
        q = pack[pl.ds(rb * RC + first // QR, rows // QR), 0:QR, :].reshape(rows, HD)
        e = jnp.exp(dot(q, keys, 1, 1) * SCALE - wide(shift[first : first + rows, :], width))
        if live is not None:
            e = jnp.where(live, e, 0.0)
        e = e.astype(BF16)
        e_out[0, row : row + rows, col : col + width] = e
        both = jnp.concatenate([values, jnp.ones_like(values)], axis=1)
        acc[first : first + rows, :] += dot(e, both, 1, 0)

    keys = pack[pl.ds(kb * KC, KC), K0:V0, :].reshape(N, HD)
    values = pack[pl.ds(kb * KC, KC), V0:P0, :].reshape(N, HD)

    @pl.when(kb < rb)
    def _():
        for first in range(0, M, FULL):
            tile(first, FULL, keys, values)

    @pl.when(kb == rb)
    def _():
        half = N // 2
        pos = row_pos(RC // 2, half, part)
        tile(0, HALF, keys[:half], values[:half], key_pos(HALF, half) <= pos)
        tile(HALF, HALF, keys, values, key_pos(HALF, N) <= wide(pos, N) + half)
        live = prefix_live(meta, HALF)
        for i in range(2):
            tile(i * HALF, HALF, pk[...], pv[...], live, (0, half + i * PTOT))
        inverse = 1.0 / acc[:, HD:]
        li_out[...] = inverse
        o_out[...] = (acc[:, :HD] * inverse).astype(BF16).reshape(RC, QR, HD)


def forward(meta, pack):
    return pl.pallas_call(
        forward_kernel,
        grid_spec=pltpu.PrefetchScalarGridSpec(
            num_scalar_prefetch=3,
            grid=(STEPS,),
            in_specs=[pl.BlockSpec((CHUNKS, PACK, HD), lambda t, r, k, m: (0, 0, 0))],
            out_specs=[
                pl.BlockSpec((1, M, N), lambda t, r, k, m: (t, 0, 0)),
                pl.BlockSpec((RC, QR, HD), lambda t, r, k, m: (r[t], 0, 0)),
                pl.BlockSpec((M, HD), lambda t, r, k, m: (r[t], 0)),
            ],
            scratch_shapes=[
                pltpu.VMEM((M, 2 * HD), F32),
                pltpu.VMEM((M, HD), F32),
                pltpu.VMEM((PTOT, HD), BF16),
                pltpu.VMEM((PTOT, HD), BF16),
                pltpu.SMEM((1,), F32),
            ],
        ),
        out_shape=[
            pltpu.HBM((STEPS, M, N), BF16),
            pltpu.HBM((CHUNKS, QR, HD), BF16),
            pltpu.HBM((N_RB * M, HD), F32),
        ],
        compiler_params=pltpu.CompilerParams(vmem_limit_bytes=VMEM),
        cost_estimate=COST(2),
        name="forward",
    )(jnp.asarray(ROW_OF), jnp.asarray(KEY_OF), meta, *in_hbm(pack))


def backward_kernel(row_of, key_of, meta, pack, d_in, e_in, o_in, li_in, dq_out, dkv_out, dq, dk, dv, dn, delta, pk, pv):
    t = pl.program_id(0)
    rb, kb = row_of[t], key_of[t]
    part = meta[SPLIT]

    @pl.when(t == 0)
    def _():
        pk[...] = prefix_rows(pack, 0)
        pv[...] = prefix_rows(pack, 1)

    @pl.when(kb == 0)
    def _():
        dq[...] = jnp.zeros_like(dq)
        d = (d_in[...].reshape(M, HD).astype(F32) * (li_in[...] * SCALE)).astype(BF16)
        dn[...] = d
        total = jnp.sum(d.astype(F32) * o_in[...].reshape(M, HD).astype(F32), axis=1, keepdims=True)
        delta[...] = jnp.broadcast_to(total, delta.shape)

    here = pl.ds(kb * N, N)

    @pl.when(rb == N_RB - 1)
    def _():
        dk[here, :] = jnp.zeros((N, HD), F32)
        dv[here, :] = jnp.zeros((N, HD), F32)

    def tile(first, rows, keys, values, at=None):
        width = keys.shape[0]
        row, col = at or (first, 0)
        d = dn[first : first + rows, :]
        e = e_in[0, row : row + rows, col : col + width]
        dp = dot(d, values, 1, 1) - wide(delta[first : first + rows, :], width)
        ds = (e.astype(F32) * dp).astype(BF16)
        dq[first : first + rows, :] += dot(ds, keys, 1, 0)
        if at is None:
            q = pack[pl.ds(rb * RC + first // QR, rows // QR), 0:QR, :].reshape(rows, HD)
            to = pl.ds(kb * N, width)
            dv[to, :] += dot(e, d, 0, 0)
            dk[to, :] += dot(ds, q, 0, 0)

    keys = pack[pl.ds(kb * KC, KC), K0:V0, :].reshape(N, HD)
    values = pack[pl.ds(kb * KC, KC), V0:P0, :].reshape(N, HD)

    @pl.when(kb < rb)
    def _():
        for first in range(0, M, FULL):
            tile(first, FULL, keys, values)

    @pl.when(kb == rb)
    def _():
        half = N // 2
        tile(0, HALF, keys[:half], values[:half])
        tile(HALF, HALF, keys, values)
        for i in range(2):
            tile(i * HALF, HALF, pk[...], pv[...], (0, half + i * PTOT))
        dq_out[...] = dq[...].astype(BF16).reshape(RC, QR, HD)
        dkv_out[:, 0:TOK, :] = dk[here, :].astype(BF16).reshape(KC, TOK, HD)
        dkv_out[:, TOK:, :] = (dv[here, :] * (1.0 / SCALE)).astype(BF16).reshape(KC, TOK, HD)


def backward(meta, pack, d, e, o, li):
    by_rows = lambda *shape: pl.BlockSpec(shape, lambda t, r, k, m: (r[t],) + (0,) * (len(shape) - 1))
    return pl.pallas_call(
        backward_kernel,
        grid_spec=pltpu.PrefetchScalarGridSpec(
            num_scalar_prefetch=3,
            grid=(STEPS,),
            in_specs=[
                pl.BlockSpec((CHUNKS, PACK, HD), lambda t, r, k, m: (0, 0, 0)),
                by_rows(RC, QR, HD),
                pl.BlockSpec((1, M, N), lambda t, r, k, m: (t, 0, 0)),
                by_rows(RC, QR, HD),
                by_rows(M, HD),
            ],
            out_specs=[
                by_rows(RC, QR, HD),
                by_rows(KC, 2 * TOK, HD),
            ],
            scratch_shapes=[
                pltpu.VMEM((M, HD), F32),
                pltpu.VMEM((CHUNKS * TOK, HD), F32),
                pltpu.VMEM((CHUNKS * TOK, HD), F32),
                pltpu.VMEM((M, HD), BF16),
                pltpu.VMEM((M, HD), F32),
                pltpu.VMEM((PTOT, HD), BF16),
                pltpu.VMEM((PTOT, HD), BF16),
            ],
        ),
        out_shape=[
            pltpu.HBM((CHUNKS, QR, HD), BF16),
            pltpu.HBM((CHUNKS, 2 * TOK, HD), BF16),
        ],
        compiler_params=pltpu.CompilerParams(vmem_limit_bytes=VMEM),
        cost_estimate=COST(4),
        name="backward",
    )(jnp.asarray(ROW_OF), jnp.asarray(KEY_OF), meta, *in_hbm(pack, d, e, o, li))


GROUPS = CHUNKS // SPLIT
AT_ONCE = 4


def cols(rows, width):
    return pl.BlockSpec((1, rows, AT_ONCE * width), lambda g: (0, 0, g))


def parts_of(rows):
    return pl.BlockSpec((SPLIT, AT_ONCE, rows, HD), lambda g: (0, g, 0, 0))


def each_head():
    for g in range(AT_ONCE):
        for h in range(GROUP):
            at = (g * GROUP + h) * HD
            yield g, slice(h * SUB, (h + 1) * SUB), slice(at, at + HD)


def gather_kernel(*refs):
    queries, rest, out = refs[0], refs[1:-1], refs[-1]
    for j in range(SPLIT):
        for g, rows, at in each_head():
            out[j, g, rows, :] = queries[0, j * SUB : (j + 1) * SUB, at]
    if rest:
        keys, values, pre_keys, pre_values = rest
        for g in range(AT_ONCE):
            at = slice(g * HD, (g + 1) * HD)
            prefix = jnp.concatenate([pre_keys[0, :, at].astype(F32), pre_values[0, :, at].astype(F32)], axis=0)
            prefix = prefix.astype(BF16)
            for j in range(SPLIT):
                out[j, g, K0:V0, :] = keys[0, :, at]
                out[j, g, V0:P0, :] = values[0, :, at]
                out[j, g, P0:PACK, :] = prefix


def gather(queries, *rest):
    rows = PACK if rest else QR
    packed = pl.pallas_call(
        gather_kernel,
        grid=(GROUPS // AT_ONCE,),
        in_specs=[cols(x.shape[1], x.shape[2] // GROUPS) for x in (queries,) + rest],
        out_specs=parts_of(rows),
        out_shape=pltpu.HBM((SPLIT, GROUPS, rows, HD), BF16),
        compiler_params=pltpu.CompilerParams(vmem_limit_bytes=VMEM),
        name="gather",
    )(*in_hbm(queries, *rest))
    return packed.reshape(CHUNKS, rows, HD)


def spread_kernel(packed, out):
    for j in range(SPLIT):
        for g, rows, at in each_head():
            out[0, j * SUB : (j + 1) * SUB, at] = packed[j, g, rows, :]


def spread(packed):
    return pl.pallas_call(
        spread_kernel,
        grid=(GROUPS // AT_ONCE,),
        in_specs=[parts_of(QR)],
        out_specs=cols(TOK, GROUP * HD),
        out_shape=pltpu.HBM((1, TOK, GROUPS * GROUP * HD), BF16),
        compiler_params=pltpu.CompilerParams(vmem_limit_bytes=VMEM),
        name="spread",
    )(*in_hbm(packed.reshape(SPLIT, GROUPS, QR, HD)))


def sum_kernel(parts, keys, values):
    for g in range(AT_ONCE):
        total = parts[0, g].astype(F32)
        for j in range(1, SPLIT):
            total += parts[j, g].astype(F32)
        keys[0, :, g * HD : (g + 1) * HD] = total[:TOK].astype(BF16)
        values[0, :, g * HD : (g + 1) * HD] = total[TOK:].astype(BF16)


def sum_parts(parts):
    shape = pltpu.HBM((1, TOK, GROUPS * HD), BF16)
    return pl.pallas_call(
        sum_kernel,
        grid=(GROUPS // AT_ONCE,),
        in_specs=[parts_of(2 * TOK)],
        out_specs=[cols(TOK, HD), cols(TOK, HD)],
        out_shape=[shape, shape],
        compiler_params=pltpu.CompilerParams(vmem_limit_bytes=VMEM),
        name="sum_parts",
    )(*in_hbm(parts.reshape(SPLIT, GROUPS, 2 * TOK, HD)))


def exchange(x):
    return lax.all_to_all(x, ("blk", "uly"), split_axis=0, concat_axis=0, tiled=True)


def shifted(block, distance):
    count = lax.axis_size("section")
    return lax.ppermute(block, "section", [((i - distance) % count, i) for i in range(count)])


def shards(queries, keys, values, pre_keys, pre_values, d_out, prefix_fill):
    part = lax.axis_index("blk").astype(jnp.int32)
    meta = jnp.concatenate([prefix_fill, part[None]])
    pack = exchange(gather(queries, keys, values, pre_keys, pre_values))
    d = exchange(gather(d_out))
    e, o, li = forward(meta, pack)
    moved_o = shifted(exchange(o), 1)
    dq, dkv = backward(meta, pack, d, e, o, li)
    moved_dq, moved_o = lax.optimization_barrier((shifted(dq, -1), moved_o))
    query_grad = spread(exchange(moved_dq))
    next_input = spread(moved_o)
    key_grad, value_grad = (shifted(x, -1) for x in sum_parts(exchange(dkv)))
    return (next_input, query_grad, key_grad, value_grad)


def solution(mesh):
    spec = P("section", ("blk", "uly"), None)
    return jax.shard_map(
        shards,
        mesh=mesh,
        in_specs=(spec,) * 6 + (P(),),
        out_specs=(spec,) * 4,
        check_vma=False,
    )
```

```python
import math

import jax
import jax.numpy as jnp
import numpy as np
from jax import lax
from jax.experimental import pallas as pl
from jax.experimental.pallas import tpu as pltpu
from jax.sharding import PartitionSpec as P

HD = 128
GROUP = 5
CHUNKS = 32
TOK = 128
SPLIT = 4
SUB = TOK // SPLIT
QR = GROUP * SUB
PRE = 8
K0, P0 = QR, QR + TOK
PACK = P0 + 2 * PRE
RC = 8
KC = 8
M = RC * QR
N = KC * TOK
HALF = M // 2
FULL = HALF
N_RB = CHUNKS // RC
PTOT = CHUNKS * PRE
SCALE = 1.0 / math.sqrt(HD)
SAFE = 60.0
NEG = -1e30
F32 = jnp.float32
BF16 = jnp.bfloat16
VMEM = 56 * 2**20

ROW_OF = np.array([r for r in reversed(range(N_RB)) for _ in range(r + 1)], np.int32)
KEY_OF = np.array([k for r in reversed(range(N_RB)) for k in range(r + 1)], np.int32)
STEPS = len(ROW_OF)


def COST(products):
    entries = STEPS * M * N
    return pl.CostEstimate(
        flops=products * 2 * entries * HD, transcendentals=entries, bytes_accessed=products * entries
    )


def in_hbm(*arrays):
    return tuple(pltpu.with_memory_space_constraint(x, pltpu.HBM) for x in arrays)


def dot(a, b, ca, cb):
    return lax.dot_general(a, b, (((ca,), (cb,)), ((), ())), preferred_element_type=F32)


def wide(x, width):
    return jnp.concatenate([x] * (width // x.shape[1]), axis=1)


def row_norm(x):
    return jnp.max(dot(x * x, jnp.ones((HD, HD), BF16), 1, 0))


def row_pos(chunks, width, part):
    shape = (chunks, GROUP, SUB, width)
    pos = lax.broadcasted_iota(jnp.int32, shape, 0) * TOK + lax.broadcasted_iota(jnp.int32, shape, 2)
    return pos.reshape(chunks * QR, width) + part * SUB


def key_pos(rows, width):
    return lax.broadcasted_iota(jnp.int32, (rows, width), 1)


def prefix_live(fill_ref, rows):
    pos = key_pos(rows, PTOT)
    live = pos < 0
    block = PTOT // SPLIT
    for b in range(SPLIT):
        live = live | ((pos >= b * block) & (pos < b * block + fill_ref[b]))
    return live


def prefix_rows(pack_ref, which):
    both = pack_ref[:, P0:PACK, :].astype(F32)
    return both[:, which * PRE : (which + 1) * PRE].reshape(PTOT, HD).astype(BF16)


def keys_and_values(part, pack, other, kall, vall):
    @pl.when(part % 2 == 0)
    def _():
        kall[...] = pack[:, K0:P0, :]
        vall[...] = other[...]

    @pl.when(part % 2 == 1)
    def _():
        kall[...] = other[...]
        vall[...] = pack[:, K0:P0, :]


def forward_kernel(row_of, key_of, meta, pack, other, e_out, o_out, li_out, acc, shift, pk, pv, kall, vall, knorm):
    t = pl.program_id(0)
    rb, kb = row_of[t], key_of[t]
    part = meta[SPLIT]

    @pl.when(t == 0)
    def _():
        pk[...] = prefix_rows(pack, 0)
        pv[...] = prefix_rows(pack, 1)
        keys_and_values(part, pack, other, kall, vall)
        knorm[0] = jnp.maximum(row_norm(pk[...]), row_norm(kall[...].reshape(CHUNKS * TOK, HD)))

    def queries():
        return pack[pl.ds(rb * RC, RC), 0:QR, :].reshape(M, HD)

    @pl.when(kb == 0)
    def _():
        acc[...] = jnp.zeros_like(acc)
        shift[...] = jnp.zeros_like(shift)
        q = queries()
        qnorm = row_norm(q)

        @pl.when(jnp.logical_not(qnorm * knorm[0] * (SCALE * SCALE) <= SAFE * SAFE))
        def _():
            live = prefix_live(meta, M)
            s = jnp.where(live, dot(q, pk[...], 1, 1) * SCALE, NEG)
            shift[...] = jnp.broadcast_to(jnp.max(s, axis=1, keepdims=True), shift.shape)

            def step(k, carry):
                keys = kall[pl.ds(k * KC, KC)].reshape(N, HD)
                pos = row_pos(RC, N, part) + rb * (RC * TOK)
                s = jnp.where(key_pos(M, N) + k * N <= pos, dot(q, keys, 1, 1) * SCALE, NEG)
                top = jnp.broadcast_to(jnp.max(s, axis=1, keepdims=True), shift.shape)
                shift[...] = jnp.maximum(shift[...], top)
                return carry

            lax.fori_loop(0, rb + 1, step, 0)

    def tile(first, rows, keys, values, live=None, at=None):
        width = keys.shape[0]
        row, col = at or (first, 0)
        q = pack[pl.ds(rb * RC + first // QR, rows // QR), 0:QR, :].reshape(rows, HD)
        e = jnp.exp(dot(q, keys, 1, 1) * SCALE - wide(shift[first : first + rows, :], width))
        if live is not None:
            e = jnp.where(live, e, 0.0)
        e = e.astype(BF16)
        e_out[0, row : row + rows, col : col + width] = e
        both = jnp.concatenate([values, jnp.ones_like(values)], axis=1)
        acc[first : first + rows, :] += dot(e, both, 1, 0)

    keys = kall[pl.ds(kb * KC, KC)].reshape(N, HD)
    values = vall[pl.ds(kb * KC, KC)].reshape(N, HD)

    @pl.when(kb < rb)
    def _():
        for first in range(0, M, FULL):
            tile(first, FULL, keys, values)

    @pl.when(kb == rb)
    def _():
        half = N // 2
        pos = row_pos(RC // 2, half, part)
        tile(0, HALF, keys[:half], values[:half], key_pos(HALF, half) <= pos)
        tile(HALF, HALF, keys, values, key_pos(HALF, N) <= wide(pos, N) + half)
        live = prefix_live(meta, HALF)
        for i in range(2):
            tile(i * HALF, HALF, pk[...], pv[...], live, (0, half + i * PTOT))
        inverse = 1.0 / acc[:, HD:]
        li_out[...] = inverse
        o_out[...] = (acc[:, :HD] * inverse).astype(BF16).reshape(RC, QR, HD)


def forward(meta, pack, other):
    return pl.pallas_call(
        forward_kernel,
        grid_spec=pltpu.PrefetchScalarGridSpec(
            num_scalar_prefetch=3,
            grid=(STEPS,),
            in_specs=[
                pl.BlockSpec((CHUNKS, PACK, HD), lambda t, r, k, m: (0, 0, 0)),
                pl.BlockSpec((CHUNKS, TOK, HD), lambda t, r, k, m: (0, 0, 0)),
            ],
            out_specs=[
                pl.BlockSpec((1, M, N), lambda t, r, k, m: (t, 0, 0)),
                pl.BlockSpec((RC, QR, HD), lambda t, r, k, m: (r[t], 0, 0)),
                pl.BlockSpec((M, HD), lambda t, r, k, m: (r[t], 0)),
            ],
            scratch_shapes=[
                pltpu.VMEM((M, 2 * HD), F32),
                pltpu.VMEM((M, HD), F32),
                pltpu.VMEM((PTOT, HD), BF16),
                pltpu.VMEM((PTOT, HD), BF16),
                pltpu.VMEM((CHUNKS, TOK, HD), BF16),
                pltpu.VMEM((CHUNKS, TOK, HD), BF16),
                pltpu.SMEM((1,), F32),
            ],
        ),
        out_shape=[
            pltpu.HBM((STEPS, M, N), BF16),
            pltpu.HBM((CHUNKS, QR, HD), BF16),
            pltpu.HBM((N_RB * M, HD), F32),
        ],
        compiler_params=pltpu.CompilerParams(vmem_limit_bytes=VMEM),
        cost_estimate=COST(2),
        name="forward",
    )(jnp.asarray(ROW_OF), jnp.asarray(KEY_OF), meta, *in_hbm(pack, other))


def backward_kernel(row_of, key_of, meta, pack, other, d_in, e_in, o_in, li_in, dq_out, keep_out, send_out, dq, dk, dv, dn, delta, pk, pv, kall, vall):
    t = pl.program_id(0)
    rb, kb = row_of[t], key_of[t]
    part = meta[SPLIT]

    @pl.when(t == 0)
    def _():
        pk[...] = prefix_rows(pack, 0)
        pv[...] = prefix_rows(pack, 1)
        keys_and_values(part, pack, other, kall, vall)

    @pl.when(kb == 0)
    def _():
        dq[...] = jnp.zeros_like(dq)
        d = (d_in[...].reshape(M, HD).astype(F32) * (li_in[...] * SCALE)).astype(BF16)
        dn[...] = d
        total = jnp.sum(d.astype(F32) * o_in[...].reshape(M, HD).astype(F32), axis=1, keepdims=True)
        delta[...] = jnp.broadcast_to(total, delta.shape)

    here = pl.ds(kb * N, N)

    @pl.when(rb == N_RB - 1)
    def _():
        dk[here, :] = jnp.zeros((N, HD), F32)
        dv[here, :] = jnp.zeros((N, HD), F32)

    def tile(first, rows, keys, values, at=None):
        width = keys.shape[0]
        row, col = at or (first, 0)
        d = dn[first : first + rows, :]
        e = e_in[0, row : row + rows, col : col + width]
        dp = dot(d, values, 1, 1) - wide(delta[first : first + rows, :], width)
        ds = (e.astype(F32) * dp).astype(BF16)
        dq[first : first + rows, :] += dot(ds, keys, 1, 0)
        if at is None:
            q = pack[pl.ds(rb * RC + first // QR, rows // QR), 0:QR, :].reshape(rows, HD)
            to = pl.ds(kb * N, width)
            dv[to, :] += dot(e, d, 0, 0)
            dk[to, :] += dot(ds, q, 0, 0)

    keys = kall[pl.ds(kb * KC, KC)].reshape(N, HD)
    values = vall[pl.ds(kb * KC, KC)].reshape(N, HD)

    @pl.when(kb < rb)
    def _():
        for first in range(0, M, FULL):
            tile(first, FULL, keys, values)

    @pl.when(kb == rb)
    def _():
        half = N // 2
        tile(0, HALF, keys[:half], values[:half])
        tile(HALF, HALF, keys, values)
        for i in range(2):
            tile(i * HALF, HALF, pk[...], pv[...], (0, half + i * PTOT))
        dq_out[...] = dq[...].astype(BF16).reshape(RC, QR, HD)
        grads_k = dk[here, :].astype(BF16).reshape(KC, TOK, HD)
        grads_v = (dv[here, :] * (1.0 / SCALE)).astype(BF16).reshape(KC, TOK, HD)

        @pl.when(part % 2 == 0)
        def _():
            keep_out[...] = grads_k
            send_out[...] = grads_v

        @pl.when(part % 2 == 1)
        def _():
            keep_out[...] = grads_v
            send_out[...] = grads_k


def backward(meta, pack, other, d, e, o, li):
    by_rows = lambda *shape: pl.BlockSpec(shape, lambda t, r, k, m: (r[t],) + (0,) * (len(shape) - 1))
    return pl.pallas_call(
        backward_kernel,
        grid_spec=pltpu.PrefetchScalarGridSpec(
            num_scalar_prefetch=3,
            grid=(STEPS,),
            in_specs=[
                pl.BlockSpec((CHUNKS, PACK, HD), lambda t, r, k, m: (0, 0, 0)),
                pl.BlockSpec((CHUNKS, TOK, HD), lambda t, r, k, m: (0, 0, 0)),
                by_rows(RC, QR, HD),
                pl.BlockSpec((1, M, N), lambda t, r, k, m: (t, 0, 0)),
                by_rows(RC, QR, HD),
                by_rows(M, HD),
            ],
            out_specs=[
                by_rows(RC, QR, HD),
                by_rows(KC, TOK, HD),
                by_rows(KC, TOK, HD),
            ],
            scratch_shapes=[
                pltpu.VMEM((M, HD), F32),
                pltpu.VMEM((CHUNKS * TOK, HD), F32),
                pltpu.VMEM((CHUNKS * TOK, HD), F32),
                pltpu.VMEM((M, HD), BF16),
                pltpu.VMEM((M, HD), F32),
                pltpu.VMEM((PTOT, HD), BF16),
                pltpu.VMEM((PTOT, HD), BF16),
                pltpu.VMEM((CHUNKS, TOK, HD), BF16),
                pltpu.VMEM((CHUNKS, TOK, HD), BF16),
            ],
        ),
        out_shape=[
            pltpu.HBM((CHUNKS, QR, HD), BF16),
            pltpu.HBM((CHUNKS, TOK, HD), BF16),
            pltpu.HBM((CHUNKS, TOK, HD), BF16),
        ],
        compiler_params=pltpu.CompilerParams(vmem_limit_bytes=VMEM),
        cost_estimate=COST(4),
        name="backward",
    )(jnp.asarray(ROW_OF), jnp.asarray(KEY_OF), meta, *in_hbm(pack, other, d, e, o, li))


GROUPS = CHUNKS // SPLIT
AT_ONCE = 4


def cols(rows, width):
    return pl.BlockSpec((1, rows, AT_ONCE * width), lambda g: (0, 0, g))


def parts_of(rows):
    return pl.BlockSpec((SPLIT, AT_ONCE, rows, HD), lambda g: (0, g, 0, 0))


def each_head():
    for g in range(AT_ONCE):
        for h in range(GROUP):
            at = (g * GROUP + h) * HD
            yield g, slice(h * SUB, (h + 1) * SUB), slice(at, at + HD)


def gather_kernel(*refs):
    queries, rest, out = refs[0], refs[1:-1], refs[-1]
    for j in range(SPLIT):
        for g, rows, at in each_head():
            out[j, g, rows, :] = queries[0, j * SUB : (j + 1) * SUB, at]
    if rest:
        keys, values, pre_keys, pre_values = rest
        for g in range(AT_ONCE):
            at = slice(g * HD, (g + 1) * HD)
            prefix = jnp.concatenate([pre_keys[0, :, at].astype(F32), pre_values[0, :, at].astype(F32)], axis=0)
            prefix = prefix.astype(BF16)
            for j in range(SPLIT):
                out[j, g, K0:P0, :] = (values if j % 2 else keys)[0, :, at]
                out[j, g, P0:PACK, :] = prefix


def gather(queries, *rest):
    rows = PACK if rest else QR
    packed = pl.pallas_call(
        gather_kernel,
        grid=(GROUPS // AT_ONCE,),
        in_specs=[cols(x.shape[1], x.shape[2] // GROUPS) for x in (queries,) + rest],
        out_specs=parts_of(rows),
        out_shape=pltpu.HBM((SPLIT, GROUPS, rows, HD), BF16),
        compiler_params=pltpu.CompilerParams(vmem_limit_bytes=VMEM),
        name="gather",
    )(*in_hbm(queries, *rest))
    return packed.reshape(CHUNKS, rows, HD)


def spread_kernel(packed, out):
    for j in range(SPLIT):
        for g, rows, at in each_head():
            out[0, j * SUB : (j + 1) * SUB, at] = packed[j, g, rows, :]


def spread(packed):
    return pl.pallas_call(
        spread_kernel,
        grid=(GROUPS // AT_ONCE,),
        in_specs=[parts_of(QR)],
        out_specs=cols(TOK, GROUP * HD),
        out_shape=pltpu.HBM((1, TOK, GROUPS * GROUP * HD), BF16),
        compiler_params=pltpu.CompilerParams(vmem_limit_bytes=VMEM),
        name="spread",
    )(*in_hbm(packed.reshape(SPLIT, GROUPS, QR, HD)))


def sum_kernel(parts, keys, values):
    for g in range(AT_ONCE):
        for first, out in ((0, keys), (1, values)):
            total = parts[first, g].astype(F32)
            for j in range(first + 2, SPLIT, 2):
                total += parts[j, g].astype(F32)
            out[0, :, g * HD : (g + 1) * HD] = total.astype(BF16)


def sum_parts(parts):
    shape = pltpu.HBM((1, TOK, GROUPS * HD), BF16)
    return pl.pallas_call(
        sum_kernel,
        grid=(GROUPS // AT_ONCE,),
        in_specs=[parts_of(TOK)],
        out_specs=[cols(TOK, HD), cols(TOK, HD)],
        out_shape=[shape, shape],
        compiler_params=pltpu.CompilerParams(vmem_limit_bytes=VMEM),
        name="sum_parts",
    )(*in_hbm(parts.reshape(SPLIT, GROUPS, TOK, HD)))


def partner(x):
    return lax.ppermute(x, "blk", [(i, i ^ 1) for i in range(lax.axis_size("blk"))])


def add_partner(keep, send):
    return (keep.astype(F32) + partner(send).astype(F32)).astype(BF16)


def exchange(x):
    return lax.all_to_all(x, ("blk", "uly"), split_axis=0, concat_axis=0, tiled=True)


def shifted(block, distance):
    count = lax.axis_size("section")
    return lax.ppermute(block, "section", [((i - distance) % count, i) for i in range(count)])


def shards(queries, keys, values, pre_keys, pre_values, d_out, prefix_fill):
    part = lax.axis_index("blk").astype(jnp.int32)
    meta = jnp.concatenate([prefix_fill, part[None]])
    pack = exchange(gather(queries, keys, values, pre_keys, pre_values))
    d = exchange(gather(d_out))
    other = partner(pack[:, K0:P0])
    e, o, li = forward(meta, pack, other)
    moved_o = shifted(exchange(o), 1)
    dq, keep, send = backward(meta, pack, other, d, e, o, li)
    moved_dq, moved_o = lax.optimization_barrier((shifted(dq, -1), moved_o))
    query_grad = spread(exchange(moved_dq))
    next_input = spread(moved_o)
    key_grad, value_grad = (shifted(x, -1) for x in sum_parts(exchange(add_partner(keep, send))))
    return (next_input, query_grad, key_grad, value_grad)


def solution(mesh):
    spec = P("section", ("blk", "uly"), None)
    return jax.shard_map(
        shards,
        mesh=mesh,
        in_specs=(spec,) * 6 + (P(),),
        out_specs=(spec,) * 4,
        check_vma=False,
    )
```

```python
import math

import jax
import jax.numpy as jnp
import numpy as np
from jax import lax
from jax.experimental import pallas as pl
from jax.experimental.pallas import tpu as pltpu
from jax.sharding import PartitionSpec as P

HD = 128
GROUP = 5
CHUNKS = 32
TOK = 128
SPLIT = 4
SUB = TOK // SPLIT
QR = GROUP * SUB
PRE = 8
K0, P0 = QR, QR + TOK
PACK = P0 + 2 * PRE
RC = 8
KC = 8
M = RC * QR
N = KC * TOK
HALF = M // 2
FULL = HALF
N_RB = CHUNKS // RC
PTOT = CHUNKS * PRE
SCALE = 1.0 / math.sqrt(HD)
SAFE = 60.0
NEG = -1e30
F32 = jnp.float32
BF16 = jnp.bfloat16
VMEM = 56 * 2**20

ROW_OF = np.array([r for r in reversed(range(N_RB)) for _ in range(r + 1)], np.int32)
KEY_OF = np.array([k for r in reversed(range(N_RB)) for k in range(r + 1)], np.int32)
STEPS = len(ROW_OF)


def COST(products):
    entries = STEPS * M * N
    return pl.CostEstimate(
        flops=products * 2 * entries * HD, transcendentals=entries, bytes_accessed=products * entries
    )


def in_hbm(*arrays):
    return tuple(pltpu.with_memory_space_constraint(x, pltpu.HBM) for x in arrays)


def dot(a, b, ca, cb):
    return lax.dot_general(a, b, (((ca,), (cb,)), ((), ())), preferred_element_type=F32)


def wide(x, width):
    return jnp.concatenate([x] * (width // x.shape[1]), axis=1)


def row_norm(x):
    return jnp.max(dot(x * x, jnp.ones((HD, HD), BF16), 1, 0))


def row_pos(chunks, width, part):
    shape = (chunks, GROUP, SUB, width)
    pos = lax.broadcasted_iota(jnp.int32, shape, 0) * TOK + lax.broadcasted_iota(jnp.int32, shape, 2)
    return pos.reshape(chunks * QR, width) + part * SUB


def key_pos(rows, width):
    return lax.broadcasted_iota(jnp.int32, (rows, width), 1)


def prefix_live(fill_ref, rows):
    pos = key_pos(rows, PTOT)
    live = pos < 0
    block = PTOT // SPLIT
    for b in range(SPLIT):
        live = live | ((pos >= b * block) & (pos < b * block + fill_ref[b]))
    return live


def prefix_rows(pack_ref, which):
    both = pack_ref[:, P0:PACK, :].astype(F32)
    return both[:, which * PRE : (which + 1) * PRE].reshape(PTOT, HD).astype(BF16)


def keys_and_values(part, pack, other, kall, vall):
    @pl.when(part % 2 == 0)
    def _():
        kall[...] = pack[:, K0:P0, :]
        vall[...] = other[...]

    @pl.when(part % 2 == 1)
    def _():
        kall[...] = other[...]
        vall[...] = pack[:, K0:P0, :]


def forward_kernel(row_of, key_of, meta, pack, other, e_out, o_out, li_out, acc, shift, pk, pv, kall, vall, knorm):
    t = pl.program_id(0)
    rb, kb = row_of[t], key_of[t]
    part = meta[SPLIT]

    @pl.when(t == 0)
    def _():
        pk[...] = prefix_rows(pack, 0)
        pv[...] = prefix_rows(pack, 1)
        keys_and_values(part, pack, other, kall, vall)
        knorm[0] = jnp.maximum(row_norm(pk[...]), row_norm(kall[...].reshape(CHUNKS * TOK, HD)))

    def queries():
        return pack[pl.ds(rb * RC, RC), 0:QR, :].reshape(M, HD)

    @pl.when(kb == 0)
    def _():
        acc[...] = jnp.zeros_like(acc)
        shift[...] = jnp.zeros_like(shift)
        q = queries()
        qnorm = row_norm(q)

        @pl.when(jnp.logical_not(qnorm * knorm[0] * (SCALE * SCALE) <= SAFE * SAFE))
        def _():
            live = prefix_live(meta, M)
            s = jnp.where(live, dot(q, pk[...], 1, 1) * SCALE, NEG)
            shift[...] = jnp.broadcast_to(jnp.max(s, axis=1, keepdims=True), shift.shape)

            def step(k, carry):
                keys = kall[pl.ds(k * KC, KC)].reshape(N, HD)
                pos = row_pos(RC, N, part) + rb * (RC * TOK)
                s = jnp.where(key_pos(M, N) + k * N <= pos, dot(q, keys, 1, 1) * SCALE, NEG)
                top = jnp.broadcast_to(jnp.max(s, axis=1, keepdims=True), shift.shape)
                shift[...] = jnp.maximum(shift[...], top)
                return carry

            lax.fori_loop(0, rb + 1, step, 0)

    def tile(first, rows, keys, values, live=None, at=None):
        width = keys.shape[0]
        row, col = at or (first, 0)
        q = pack[pl.ds(rb * RC + first // QR, rows // QR), 0:QR, :].reshape(rows, HD)
        e = jnp.exp(dot(q, keys, 1, 1) * SCALE - wide(shift[first : first + rows, :], width))
        if live is not None:
            e = jnp.where(live, e, 0.0)
        e = e.astype(BF16)
        e_out[0, row : row + rows, col : col + width] = e
        both = jnp.concatenate([values, jnp.ones_like(values)], axis=1)
        acc[first : first + rows, :] += dot(e, both, 1, 0)

    keys = kall[pl.ds(kb * KC, KC)].reshape(N, HD)
    values = vall[pl.ds(kb * KC, KC)].reshape(N, HD)

    @pl.when(kb < rb)
    def _():
        for first in range(0, M, FULL):
            tile(first, FULL, keys, values)

    @pl.when(kb == rb)
    def _():
        half = N // 2
        pos = row_pos(RC // 2, half, part)
        tile(0, HALF, keys[:half], values[:half], key_pos(HALF, half) <= pos)
        tile(HALF, HALF, keys, values, key_pos(HALF, N) <= wide(pos, N) + half)
        live = prefix_live(meta, HALF)
        for i in range(2):
            tile(i * HALF, HALF, pk[...], pv[...], live, (0, half + i * PTOT))
        inverse = 1.0 / acc[:, HD:]
        li_out[...] = inverse
        o_out[...] = (acc[:, :HD] * inverse).astype(BF16).reshape(RC, QR, HD)


def forward(meta, pack, other):
    return pl.pallas_call(
        forward_kernel,
        grid_spec=pltpu.PrefetchScalarGridSpec(
            num_scalar_prefetch=3,
            grid=(STEPS,),
            in_specs=[
                pl.BlockSpec((CHUNKS, PACK, HD), lambda t, r, k, m: (0, 0, 0)),
                pl.BlockSpec((CHUNKS, TOK, HD), lambda t, r, k, m: (0, 0, 0)),
            ],
            out_specs=[
                pl.BlockSpec((1, M, N), lambda t, r, k, m: (t, 0, 0)),
                pl.BlockSpec((RC, QR, HD), lambda t, r, k, m: (r[t], 0, 0)),
                pl.BlockSpec((M, HD), lambda t, r, k, m: (r[t], 0)),
            ],
            scratch_shapes=[
                pltpu.VMEM((M, 2 * HD), F32),
                pltpu.VMEM((M, HD), F32),
                pltpu.VMEM((PTOT, HD), BF16),
                pltpu.VMEM((PTOT, HD), BF16),
                pltpu.VMEM((CHUNKS, TOK, HD), BF16),
                pltpu.VMEM((CHUNKS, TOK, HD), BF16),
                pltpu.SMEM((1,), F32),
            ],
        ),
        out_shape=[
            pltpu.HBM((STEPS, M, N), BF16),
            pltpu.HBM((CHUNKS, QR, HD), BF16),
            pltpu.HBM((N_RB * M, HD), F32),
        ],
        compiler_params=pltpu.CompilerParams(vmem_limit_bytes=VMEM),
        cost_estimate=COST(2),
        name="forward",
    )(jnp.asarray(ROW_OF), jnp.asarray(KEY_OF), meta, *in_hbm(pack, other))


def backward_kernel(row_of, key_of, meta, pack, other, d_in, e_in, o_in, li_in, dq_out, keep_out, send_out, dq, dk, dv, dn, delta, pk, pv, kall, vall):
    t = pl.program_id(0)
    rb, kb = row_of[t], key_of[t]
    part = meta[SPLIT]

    @pl.when(t == 0)
    def _():
        pk[...] = prefix_rows(pack, 0)
        pv[...] = prefix_rows(pack, 1)
        keys_and_values(part, pack, other, kall, vall)

    @pl.when(kb == 0)
    def _():
        dq[...] = jnp.zeros_like(dq)
        d = (d_in[...].reshape(M, HD).astype(F32) * (li_in[...] * SCALE)).astype(BF16)
        dn[...] = d
        total = jnp.sum(d.astype(F32) * o_in[...].reshape(M, HD).astype(F32), axis=1, keepdims=True)
        delta[...] = jnp.broadcast_to(total, delta.shape)

    here = pl.ds(kb * N, N)

    @pl.when(rb == N_RB - 1)
    def _():
        dk[here, :] = jnp.zeros((N, HD), F32)
        dv[here, :] = jnp.zeros((N, HD), F32)

    def tile(first, rows, keys, values, at=None):
        width = keys.shape[0]
        row, col = at or (first, 0)
        d = dn[first : first + rows, :]
        e = e_in[0, row : row + rows, col : col + width]
        dp = dot(d, values, 1, 1) - wide(delta[first : first + rows, :], width)
        ds = (e.astype(F32) * dp).astype(BF16)
        dq[first : first + rows, :] += dot(ds, keys, 1, 0)
        if at is None:
            q = pack[pl.ds(rb * RC + first // QR, rows // QR), 0:QR, :].reshape(rows, HD)
            to = pl.ds(kb * N, width)
            dv[to, :] += dot(e, d, 0, 0)
            dk[to, :] += dot(ds, q, 0, 0)

    keys = kall[pl.ds(kb * KC, KC)].reshape(N, HD)
    values = vall[pl.ds(kb * KC, KC)].reshape(N, HD)

    @pl.when(kb < rb)
    def _():
        for first in range(0, M, FULL):
            tile(first, FULL, keys, values)

    @pl.when(kb == rb)
    def _():
        half = N // 2
        tile(0, HALF, keys[:half], values[:half])
        tile(HALF, HALF, keys, values)
        for i in range(2):
            tile(i * HALF, HALF, pk[...], pv[...], (0, half + i * PTOT))
        dq_out[...] = dq[...].astype(BF16).reshape(RC, QR, HD)
        grads_k = dk[here, :].astype(BF16).reshape(KC, TOK, HD)
        grads_v = (dv[here, :] * (1.0 / SCALE)).astype(BF16).reshape(KC, TOK, HD)

        @pl.when(part % 2 == 0)
        def _():
            keep_out[...] = grads_k
            send_out[...] = grads_v

        @pl.when(part % 2 == 1)
        def _():
            keep_out[...] = grads_v
            send_out[...] = grads_k


def backward(meta, pack, other, d, e, o, li):
    by_rows = lambda *shape: pl.BlockSpec(shape, lambda t, r, k, m: (r[t],) + (0,) * (len(shape) - 1))
    return pl.pallas_call(
        backward_kernel,
        grid_spec=pltpu.PrefetchScalarGridSpec(
            num_scalar_prefetch=3,
            grid=(STEPS,),
            in_specs=[
                pl.BlockSpec((CHUNKS, PACK, HD), lambda t, r, k, m: (0, 0, 0)),
                pl.BlockSpec((CHUNKS, TOK, HD), lambda t, r, k, m: (0, 0, 0)),
                by_rows(RC, QR, HD),
                pl.BlockSpec((1, M, N), lambda t, r, k, m: (t, 0, 0)),
                by_rows(RC, QR, HD),
                by_rows(M, HD),
            ],
            out_specs=[
                by_rows(RC, QR, HD),
                by_rows(KC, TOK, HD),
                by_rows(KC, TOK, HD),
            ],
            scratch_shapes=[
                pltpu.VMEM((M, HD), F32),
                pltpu.VMEM((CHUNKS * TOK, HD), F32),
                pltpu.VMEM((CHUNKS * TOK, HD), F32),
                pltpu.VMEM((M, HD), BF16),
                pltpu.VMEM((M, HD), F32),
                pltpu.VMEM((PTOT, HD), BF16),
                pltpu.VMEM((PTOT, HD), BF16),
                pltpu.VMEM((CHUNKS, TOK, HD), BF16),
                pltpu.VMEM((CHUNKS, TOK, HD), BF16),
            ],
        ),
        out_shape=[
            pltpu.HBM((CHUNKS, QR, HD), BF16),
            pltpu.HBM((CHUNKS, TOK, HD), BF16),
            pltpu.HBM((CHUNKS, TOK, HD), BF16),
        ],
        compiler_params=pltpu.CompilerParams(vmem_limit_bytes=VMEM),
        cost_estimate=COST(4),
        name="backward",
    )(jnp.asarray(ROW_OF), jnp.asarray(KEY_OF), meta, *in_hbm(pack, other, d, e, o, li))


GROUPS = CHUNKS // SPLIT
AT_ONCE = 8


def cols(rows, width):
    return pl.BlockSpec((1, rows, AT_ONCE * width), lambda g: (0, 0, g))


def parts_of(rows):
    return pl.BlockSpec((SPLIT, AT_ONCE, rows, HD), lambda g: (0, g, 0, 0))


def each_head():
    for g in range(AT_ONCE):
        for h in range(GROUP):
            at = (g * GROUP + h) * HD
            yield g, slice(h * SUB, (h + 1) * SUB), slice(at, at + HD)


def gather_kernel(*refs):
    queries, rest, out = refs[0], refs[1:-1], refs[-1]
    for j in range(SPLIT):
        for g, rows, at in each_head():
            out[j, g, rows, :] = queries[0, j * SUB : (j + 1) * SUB, at]
    if rest:
        keys, values, pre_keys, pre_values = rest
        for g in range(AT_ONCE):
            at = slice(g * HD, (g + 1) * HD)
            prefix = jnp.concatenate([pre_keys[0, :, at].astype(F32), pre_values[0, :, at].astype(F32)], axis=0)
            prefix = prefix.astype(BF16)
            for j in range(SPLIT):
                out[j, g, K0:P0, :] = (values if j % 2 else keys)[0, :, at]
                out[j, g, P0:PACK, :] = prefix


def gather(queries, *rest):
    rows = PACK if rest else QR
    packed = pl.pallas_call(
        gather_kernel,
        grid=(GROUPS // AT_ONCE,),
        in_specs=[cols(x.shape[1], x.shape[2] // GROUPS) for x in (queries,) + rest],
        out_specs=parts_of(rows),
        out_shape=pltpu.HBM((SPLIT, GROUPS, rows, HD), BF16),
        compiler_params=pltpu.CompilerParams(vmem_limit_bytes=VMEM),
        name="gather",
    )(*in_hbm(queries, *rest))
    return packed.reshape(CHUNKS, rows, HD)


def spread_kernel(packed, out):
    for j in range(SPLIT):
        for g, rows, at in each_head():
            out[0, j * SUB : (j + 1) * SUB, at] = packed[j, g, rows, :]


def spread(packed):
    return pl.pallas_call(
        spread_kernel,
        grid=(GROUPS // AT_ONCE,),
        in_specs=[parts_of(QR)],
        out_specs=cols(TOK, GROUP * HD),
        out_shape=pltpu.HBM((1, TOK, GROUPS * GROUP * HD), BF16),
        compiler_params=pltpu.CompilerParams(vmem_limit_bytes=VMEM),
        name="spread",
    )(*in_hbm(packed.reshape(SPLIT, GROUPS, QR, HD)))


def sum_kernel(parts, keys, values):
    for g in range(AT_ONCE):
        for first, out in ((0, keys), (1, values)):
            total = parts[first, g].astype(F32)
            for j in range(first + 2, SPLIT, 2):
                total += parts[j, g].astype(F32)
            out[0, :, g * HD : (g + 1) * HD] = total.astype(BF16)


def sum_parts(parts):
    shape = pltpu.HBM((1, TOK, GROUPS * HD), BF16)
    return pl.pallas_call(
        sum_kernel,
        grid=(GROUPS // AT_ONCE,),
        in_specs=[parts_of(TOK)],
        out_specs=[cols(TOK, HD), cols(TOK, HD)],
        out_shape=[shape, shape],
        compiler_params=pltpu.CompilerParams(vmem_limit_bytes=VMEM),
        name="sum_parts",
    )(*in_hbm(parts.reshape(SPLIT, GROUPS, TOK, HD)))


def partner(x):
    return lax.ppermute(x, "blk", [(i, i ^ 1) for i in range(lax.axis_size("blk"))])


def add_partner(keep, send):
    return (keep.astype(F32) + partner(send).astype(F32)).astype(BF16)


def exchange(x):
    return lax.all_to_all(x, ("blk", "uly"), split_axis=0, concat_axis=0, tiled=True)


def shifted(block, distance):
    count = lax.axis_size("section")
    return lax.ppermute(block, "section", [((i - distance) % count, i) for i in range(count)])


def shards(queries, keys, values, pre_keys, pre_values, d_out, prefix_fill):
    part = lax.axis_index("blk").astype(jnp.int32)
    meta = jnp.concatenate([prefix_fill, part[None]])
    pack = exchange(gather(queries, keys, values, pre_keys, pre_values))
    d = exchange(gather(d_out))
    other = partner(pack[:, K0:P0])
    e, o, li = forward(meta, pack, other)
    moved_o = shifted(exchange(o), 1)
    dq, keep, send = backward(meta, pack, other, d, e, o, li)
    moved_dq, moved_o = lax.optimization_barrier((shifted(dq, -1), moved_o))
    query_grad = spread(exchange(moved_dq))
    next_input = spread(moved_o)
    key_grad, value_grad = (shifted(x, -1) for x in sum_parts(exchange(add_partner(keep, send))))
    return (next_input, query_grad, key_grad, value_grad)


def solution(mesh):
    spec = P("section", ("blk", "uly"), None)
    return jax.shard_map(
        shards,
        mesh=mesh,
        in_specs=(spec,) * 6 + (P(),),
        out_specs=(spec,) * 4,
        check_vma=False,
    )
```
